32 devices in a mesh: row: 8 (over z, core), col: 4 (over y, x).
Axes of the slice: x: 2, y: 2, z: 4, core: 2. Of those that a mesh axis runs over, the one named last changes fastest.
Arguments:
- panel_diag: float32 [512, 512], P('row'), may hold values from -12 to 150, as said below
- panel_below: float32 [4096, 512], P(('row', 'col')), may hold values from -6 to 6
- trailing: float32 [4096, 4096], P('row', 'col'), may hold values from -6 to 6
- recon_top: float32 [512, 12288], P(None, 'col'), may hold values from -6 to 6
- recon_rest: float32 [4096, 12288], P('row', 'col'), may hold values from -6 to 6
Outputs:
- diag_factor: float32 [512, 512], replicated
- below_factor: float32 [4096, 512], P(('row', 'col'))
- trailing_new: float32 [4096, 4096], P('row', 'col')
- top_solved: float32 [512, 12288], P(None, 'col')
- rest_new: float32 [4096, 12288], P('row', 'col')
The draws below stay inside these ranges and needn't reach their ends.
Inputs may be any that keep to these rules, and one draw needn't show every extreme that they name: panel_diag is symmetric with a positive diagonal that dominates its spectrum, so it is positive definite.
All inputs are finite; a program needn't handle non-finite values.
Results may differ from the reference program's by a relative error of at most 0.00007.
Values sent between devices are 32-bit elements; how exact they have to be, the bound alone decides.
A program may use at most 128 MiB of HBM per device.

```python
import jax
import jax.numpy as jnp
from jax import lax

NB = 512
KS = 12288
MT = 4096


def draw_panel_diag(key, part):
    first_key, second_key = jax.random.split(jax.random.fold_in(key, 17))
    base = jax.random.normal(first_key, (NB, NB), jnp.float32)
    symmetric = (base + base.T) * 0.7071
    symmetric = jnp.clip(symmetric, -12.0, 12.0)
    spread = jax.random.uniform(second_key, (NB,), jnp.float32, 0.0, 0.5)
    diagonal = 96.0 * (1.0 + spread)
    identity = (jnp.arange(NB)[:, None] == jnp.arange(NB)[None, :]).astype(jnp.float32)
    return symmetric * (1.0 - identity) + identity * diagonal[None, :]


def shard_levels(rng, dims, pieces, least, high):
    def one(position, shards_of):
        heights = jax.random.uniform(jax.random.fold_in(jax.random.fold_in(rng, 6), position), (shards_of,), jnp.float32, least / len(pieces), high / len(pieces))
        return jnp.repeat(jnp.exp(heights), dims[position] // shards_of).reshape((-1,) + (1,) * (len(dims) - position - 1))

    factor_of = one(*pieces[0])
    for cut in pieces[1:]:
        factor_of = factor_of * one(*cut)
    return factor_of


def centred(stream_key, extent, scale, most, cuts=(), kind=jnp.bfloat16):
    drawn = scale * jax.random.normal(stream_key, extent, jnp.float32)
    if cuts:
        drawn = drawn * shard_levels(stream_key, extent, cuts, -0.22, 0.18)
    return jnp.clip(drawn, -most, most).astype(kind)


def setup_inputs(seed: int = 0) -> dict:
    streams_of = jax.random.split(jax.random.key(seed), 6)
    panel_diag = draw_panel_diag(jax.random.fold_in(streams_of[5], 71), 0)
    panel_below = centred(streams_of[1], (MT, NB), 1.0, 6.0, ((0, 32),), jnp.float32)
    trailing = centred(streams_of[2], (MT, MT), 1.0, 6.0, ((0, 8), (1, 4)), jnp.float32)
    recon_top = centred(streams_of[3], (NB, KS), 1.0, 6.0, ((1, 4),), jnp.float32)
    recon_rest = centred(streams_of[4], (MT, KS), 1.0, 6.0, ((0, 8), (1, 4)), jnp.float32)
    return {"panel_diag": panel_diag, "panel_below": panel_below, "trailing": trailing, "recon_top": recon_top, "recon_rest": recon_rest}


def reference(panel_diag, panel_below, trailing, recon_top, recon_rest):
    diag_factor = jnp.linalg.cholesky(panel_diag)
    below_factor = jax.scipy.linalg.solve_triangular(diag_factor, panel_below.T, lower=True).T
    product = jnp.dot(below_factor, below_factor.T, precision=lax.Precision.HIGHEST)
    row_index = jnp.arange(MT, dtype=jnp.int32)[:, None]
    col_index = jnp.arange(MT, dtype=jnp.int32)[None, :]
    trailing_new = jnp.where(col_index <= row_index, trailing - product, trailing)
    top_solved = jax.scipy.linalg.solve_triangular(diag_factor, recon_top, lower=True)
    rest_new = recon_rest - jnp.dot(below_factor, top_solved, precision=lax.Precision.HIGHEST)
    return (diag_factor, below_factor, trailing_new, top_solved, rest_new)
```

```python
import functools

import jax
import jax.numpy as jnp
from jax import lax
from jax.experimental import pallas as pl
from jax.experimental.pallas import tpu as pltpu
from jax.sharding import PartitionSpec as P

HI = lax.Precision.HIGHEST
MESH = pl.DeviceIdType.MESH
BLOCK = 128
SUB = 8


def mm(a, b, dims, precision=HI):
    return lax.dot_general(a, b, (dims, ((), ())), precision=precision, preferred_element_type=jnp.float32)

def factor_block(mat, tick):
    row_id = lax.broadcasted_iota(jnp.int32, (SUB, BLOCK), 0)
    lane_id = lax.broadcasted_iota(jnp.int32, (SUB, BLOCK), 1)
    steps = BLOCK // SUB
    d = mat
    uppers, invs = [], []
    g = None
    for s in range(steps):
        base = s * SUB
        rows = d[:SUB, :]
        eye = jnp.where(lane_id == row_id + base, 1.0, 0.0).astype(jnp.float32)
        if g is None:
            grows = eye
        else:
            grows = g[:SUB, :] + eye
        r = [jnp.broadcast_to(rows[j:j+1, :], (SUB, BLOCK)) for j in range(SUB)]
        q = [jnp.broadcast_to(grows[j:j+1, :], (SUB, BLOCK)) for j in range(SUB)]
        S = {}
        for j in range(SUB):
            for k in range(j, SUB):
                S[j, k] = jnp.broadcast_to(r[j][:, base+k:base+k+1], (SUB, BLOCK))
        for j in range(SUB):
            inv = lax.rsqrt(S[j, j])
            c = [None] * SUB
            for k in range(j + 1, SUB):
                c[k] = S[j, k] * inv
            r[j] = r[j] * inv
            q[j] = q[j] * inv
            for i in range(j + 1, SUB):
                for k in range(i, SUB):
                    S[i, k] = S[i, k] - c[i] * c[k]
                r[i] = r[i] - c[i] * r[j]
                q[i] = q[i] - c[i] * q[j]
        u = r[0]
        v = q[0]
        for j in range(1, SUB):
            u = jnp.where(row_id == j, r[j], u)
            v = jnp.where(row_id == j, q[j], v)
        u = jnp.where(lane_id >= row_id + base, u, 0.0)
        uppers.append(u)
        invs.append(v)
        tick()
        if s + 1 < steps:
            both = jnp.concatenate([u, v], axis=1)
            upd = mm(u, both, ((0,), (0,)))
            d = d[SUB:, :] - upd[base+SUB:, :BLOCK]
            g = -upd[base+SUB:, BLOCK:] if g is None else g[SUB:, :] - upd[base+SUB:, BLOCK:]
    return jnp.concatenate(uppers, 0), jnp.concatenate(invs, 0)


def factor_kernel(rows_n, cols_n, a_ref, pb_ref, l_ref, inv_ref, pr_ref, pc_ref, w, y,
                  d_send, d_recv, x_send, x_recv, s_send, s_recv, c_send, c_recv, b_send, b_recv):
    n = w.shape[0]
    chips = rows_n // 2
    piece = n // rows_n
    tall = pb_ref.shape[0]
    block_rows = pr_ref.shape[0]
    ratio = pc_ref.shape[0] // block_rows
    r = lax.axis_index("row")
    c = lax.axis_index("col")
    z = r // 2
    k = lax.rem(r, 2)
    sibling = z * 2 + (1 - k)

    barrier = pltpu.get_barrier_semaphore()
    for step in range(1, rows_n):
        pl.semaphore_signal(barrier, inc=1, device_id=(lax.rem(r + step, rows_n), c), device_id_type=MESH)
    for step in range(1, cols_n):
        pl.semaphore_signal(barrier, inc=1, device_id=(r, lax.rem(c + step, cols_n)), device_id_type=MESH)
    w[pl.ds(pl.multiple_of(r * piece, piece), piece), :] = a_ref[...]
    pr_ref[pl.ds(pl.multiple_of(c * tall, tall), tall), :] = pb_ref[...]
    pl.semaphore_wait(barrier, rows_n + cols_n - 2)

    messages = []
    for p in range(chips):
        lo = p * 2 * piece // BLOCK * BLOCK
        if p == 0:
            messages.append((0, 0, BLOCK))
            lo = BLOCK
        if lo < n:
            messages.append((p, lo, n))

    def diag_copy(m, row, to_row, send, recv):
        p, lo, hi = messages[m]
        part = w.at[pl.ds(pl.multiple_of(row * piece, piece), piece), lo:hi]
        return pltpu.make_async_remote_copy(src_ref=part, dst_ref=part, send_sem=send, recv_sem=recv,
                                            device_id=(to_row, c), device_id_type=MESH)

    def along(m, step):
        to = lax.rem(z + step, chips) * 2 + k
        return diag_copy(m, r, to, d_send.at[m, step - 1], d_recv.at[m])

    def across(m):
        return diag_copy(m, messages[m][0] * 2 + k, sibling, x_send.at[m], x_recv.at[m])

    for m in range(len(messages)):
        @pl.when(z == messages[m][0])
        def _():
            for step in range(1, chips):
                along(m, step).start()

    passed = set()

    def pass_across(m):
        if m in passed:
            return
        passed.add(m)

        @pl.when(z != messages[m][0])
        def _():
            diag_copy(m, messages[m][0] * 2 + k, sibling, d_send.at[m, 0], d_recv.at[m]).wait_recv()
        across(m).start()

    def have(m):
        pass_across(m)
        part = diag_copy(m, messages[m][0] * 2 + (1 - k), sibling, x_send.at[m], x_recv.at[m])
        part.wait_recv()

    def in_row(step):
        part = pr_ref.at[pl.ds(pl.multiple_of(c * tall, tall), tall)]
        return pltpu.make_async_remote_copy(
            src_ref=part, dst_ref=part, send_sem=s_send.at[step - 1], recv_sem=s_recv.at[step - 1],
            device_id=(r, lax.rem(c - step + cols_n, cols_n)), device_id_type=MESH)

    def in_row_wait(step):
        part = pr_ref.at[pl.ds(pl.multiple_of(lax.rem(c + step, cols_n) * tall, tall), tall)]
        pltpu.make_async_remote_copy(
            src_ref=part, dst_ref=part, send_sem=s_send.at[step - 1], recv_sem=s_recv.at[step - 1],
            device_id=(r, lax.rem(c + step, cols_n)), device_id_type=MESH).wait_recv()

    home = c * ratio // 2

    def piece_at(j, core):
        first = lax.rem(c + j, cols_n) * tall
        base = core * block_rows if ratio == 2 else 0
        return pl.multiple_of(base + first, tall)

    def line_copy(j, to, send, recv, core):
        part = pc_ref.at[pl.ds(piece_at(j, core), tall)]
        return pltpu.make_async_remote_copy(src_ref=part, dst_ref=part, send_sem=send, recv_sem=recv,
                                            device_id=(to, c), device_id_type=MESH)

    def down(j):
        return line_copy(j, r + 2, c_send.at[j], c_recv.at[j], k)

    def swap(j, core):
        return line_copy(j, sibling, b_send.at[j], b_recv.at[j], core)

    holds = (z >= home) if ratio == 2 else (z >= home) & (lax.rem(c, 2) == k)
    takes = (z >= home) if ratio == 2 else (z >= home) & (lax.rem(c, 2) != k)

    def line_step(j, hop):
        @pl.when((z - home == hop) & holds)
        def _():
            if hop == 0:
                first = pl.multiple_of(lax.rem(c + j, cols_n) * tall, tall)
                pc_ref[pl.ds(piece_at(j, k), tall), :] = pr_ref[pl.ds(first, tall), :]
            else:
                down(j).wait_recv()
            @pl.when(z < chips - 1)
            def _():
                down(j).start()
            swap(j, k).start()

    ticks = n // SUB
    actions = {}
    span = cols_n + chips - 1
    for m in range(1, len(messages)):
        actions.setdefault(4 * m - 1, []).append(functools.partial(pass_across, m))
    for t in range(span):
        at = 2 + t * (ticks - 8) // (span - 1)
        if 0 < t < cols_n:
            actions.setdefault(at, []).append(functools.partial(in_row_wait, t))
        for j in range(cols_n):
            hop = t - j
            if 0 <= hop < chips:
                actions.setdefault(at, []).append(functools.partial(line_step, j, hop))
    count = [0]

    def tick():
        for action in actions.get(count[0], ()):
            action()
        count[0] += 1

    pass_across(0)
    for step in range(1, cols_n):
        in_row(step).start()
    y[...] = jnp.zeros_like(y)
    l_ref[...] = jnp.zeros_like(l_ref)
    have(0)
    waited = {0}
    for p in range(n // BLOCK):
        lo, hi = p * BLOCK, (p + 1) * BLOCK
        for m in range(len(messages)):
            if m not in waited and messages[m][0] * 2 * piece < hi and (p or messages[m][1] == 0):
                have(m)
                waited.add(m)
        now = w[lo:hi, lo:] if p else w[lo:hi, lo:hi]
        if p:
            before = l_ref[lo:, :lo]
            now = now - mm(l_ref[lo:hi, :lo], before, ((1,), (1,)))
        u, v = factor_block(now[:, :BLOCK], tick)
        l_ref[lo:hi, lo:hi] = u.T
        if p:
            left = mm(l_ref[lo:hi, :lo], y[:lo, :lo], ((1,), (0,)))
            y[lo:hi, :lo] = -mm(v, left, ((1,), (0,)))
        y[lo:hi, lo:hi] = v
        if hi < n:
            if p == 0:
                for m in range(len(messages)):
                    if m not in waited and messages[m][0] * 2 * piece < hi:
                        have(m)
                        waited.add(m)
                rest = w[lo:hi, hi:]
            else:
                rest = now[:, BLOCK:]
            l_ref[hi:, lo:hi] = mm(v, rest, ((1,), (0,))).T
    inv_ref[...] = y[...]

    for m in range(len(messages)):
        @pl.when(z == messages[m][0])
        def _():
            for step in range(1, chips):
                along(m, step).wait_send()
        across(m).wait_send()
    for step in range(1, cols_n):
        in_row(step).wait_send()
    for j in range(cols_n):
        @pl.when(holds)
        def _():
            @pl.when(z < chips - 1)
            def _():
                down(j).wait_send()
            swap(j, k).wait_send()

        @pl.when(takes)
        def _():
            swap(j, 1 - k).wait_recv()


def split(x):
    high = x.astype(jnp.bfloat16)
    return high, (x - high.astype(jnp.float32)).astype(jnp.bfloat16)


def dot3(a, b, dims):
    def one(p, q):
        return lax.dot_general(p, q, (dims, ((), ())), preferred_element_type=jnp.float32)
    return one(a[0], b[0]) + (one(a[0], b[1]) + one(a[1], b[0]))


ROWS = ((1,), (0,))
COLS = ((1,), (1,))


def update_kernel(wide, deep, pr_ref, pc_ref, inv_ref, pb_ref, top_ref, rest_ref, tr_ref,
                  below_ref, top_out, rest_out, tr_out, xr_hi, xr_lo, xc_hi, xc_lo, iv_hi, iv_lo):
    t = pl.program_id(0)
    r = lax.axis_index("row")
    c = lax.axis_index("col")

    @pl.when(t == 0)
    def _():
        inv = split(inv_ref[...])
        iv_hi[...], iv_lo[...] = inv
        xr_hi[...], xr_lo[...] = split(dot3(split(pr_ref[...]), inv, COLS))
        xc_hi[...], xc_lo[...] = split(dot3(split(pc_ref[...]), inv, COLS))
        below_ref[...] = dot3(split(pb_ref[...]), inv, COLS)

    @pl.when(t < wide)
    def _():
        n = inv_ref.shape[0]
        half = n // 2
        top = split(top_ref[...])
        upper = dot3((iv_hi[:half, :half], iv_lo[:half, :half]), (top[0][:half], top[1][:half]), ROWS)
        lower = dot3((iv_hi[half:, :], iv_lo[half:, :]), top, ROWS)
        top_out[:half, :] = upper
        top_out[half:, :] = lower
        solved = split(jnp.concatenate([upper, lower], 0))
        rest_out[...] = rest_ref[...] - dot3((xr_hi[...], xr_lo[...]), solved, ROWS)

    @pl.when(t >= wide)
    def _():
        height, width = tr_ref.shape
        at = pl.ds(pl.multiple_of((t - wide) * width, width), width)
        product = dot3((xr_hi[...], xr_lo[...]), (xc_hi[at, :], xc_lo[at, :]), COLS)
        row = r * height + lax.broadcasted_iota(jnp.int32, (height, width), 0)
        col = (c * deep + (t - wide)) * width + lax.broadcasted_iota(jnp.int32, (height, width), 1)
        tr_out[...] = jnp.where(col <= row, tr_ref[...] - product, tr_ref[...])


def tile_of(size):
    for width in (512, 384, 256, 128):
        if size % width == 0:
            return width
    return size


def shards(rows_n, cols_n, panel_diag, panel_below, trailing, recon_top, recon_rest):
    n = panel_diag.shape[1]
    height, across = trailing.shape
    slopes = recon_top.shape[1]
    f32 = jnp.float32
    whole = pl.BlockSpec(memory_space=pltpu.VMEM)
    chips = rows_n // 2
    dma = pltpu.SemaphoreType.DMA
    diag_factor, inverse, row_panel, col_panel = pl.pallas_call(
        functools.partial(factor_kernel, rows_n, cols_n),
        out_shape=[jax.ShapeDtypeStruct((n, n), f32), jax.ShapeDtypeStruct((n, n), f32),
                   jax.ShapeDtypeStruct((height, n), f32), jax.ShapeDtypeStruct((across, n), f32)],
        in_specs=[whole] * 2,
        out_specs=[whole] * 4,
        scratch_shapes=[pltpu.VMEM((n, n), f32), pltpu.VMEM((n, n), f32),
                        dma((chips + 1, chips - 1)), dma((chips + 1,)), dma((chips + 1,)), dma((chips + 1,)),
                        dma((cols_n - 1,)), dma((cols_n - 1,)), dma((cols_n,)), dma((cols_n,)),
                        dma((cols_n,)), dma((cols_n,))],
        compiler_params=pltpu.CompilerParams(collective_id=0, has_side_effects=True, vmem_limit_bytes=48 * 2**20),
        name="factor",
    )(panel_diag, panel_below)

    tile, strip = tile_of(slopes), tile_of(across)
    wide, deep = slopes // tile, across // strip
    bf16 = jnp.bfloat16
    recon_at = lambda t: (0, jnp.minimum(t, wide - 1))
    trail_at = lambda t: (0, jnp.maximum(t - wide, 0))
    below, top_solved, rest_new, trailing_new = pl.pallas_call(
        functools.partial(update_kernel, wide, deep),
        grid=(wide + deep,),
        out_shape=[jax.ShapeDtypeStruct(panel_below.shape, f32), jax.ShapeDtypeStruct(recon_top.shape, f32),
                   jax.ShapeDtypeStruct(recon_rest.shape, f32), jax.ShapeDtypeStruct(trailing.shape, f32)],
        in_specs=[whole, whole, whole, whole, pl.BlockSpec((n, tile), recon_at),
                  pl.BlockSpec((height, tile), recon_at), pl.BlockSpec((height, strip), trail_at)],
        out_specs=[whole, pl.BlockSpec((n, tile), recon_at),
                   pl.BlockSpec((height, tile), recon_at), pl.BlockSpec((height, strip), trail_at)],
        scratch_shapes=[pltpu.VMEM((height, n), bf16), pltpu.VMEM((height, n), bf16),
                        pltpu.VMEM((across, n), bf16), pltpu.VMEM((across, n), bf16),
                        pltpu.VMEM((n, n), bf16), pltpu.VMEM((n, n), bf16)],
        compiler_params=pltpu.CompilerParams(vmem_limit_bytes=50 * 2**20),
        name="update",
    )(row_panel, col_panel, inverse, panel_below, recon_top, recon_rest, trailing)
    return (diag_factor, below, trailing_new, top_solved, rest_new)


def solution(mesh):
    rows_n, cols_n = mesh.shape["row"], mesh.shape["col"]
    placed = (
        P("row", None),
        P(("row", "col"), None),
        P("row", "col"),
        P(None, "col"),
        P("row", "col"),
    )
    return jax.shard_map(
        functools.partial(shards, rows_n, cols_n),
        mesh=mesh,
        in_specs=placed,
        out_specs=(P(), P(("row", "col"), None), P("row", "col"), P(None, "col"), P("row", "col")),
        check_vma=False,
    )
```

```python
import functools

import jax
import jax.numpy as jnp
from jax import lax
from jax.experimental import pallas as pl
from jax.experimental.pallas import tpu as pltpu
from jax.sharding import PartitionSpec as P

HI = lax.Precision.HIGHEST
MESH = pl.DeviceIdType.MESH
BLOCK = 128
SUB = 8


def rounded(x):
    return x.astype(jnp.bfloat16).astype(jnp.float32)

def mm6(a, b, dims):
    def parts(x):
        high = rounded(x)
        mid = rounded(x - high)
        return high, mid, (x - high) - mid
    ah, am, al = parts(a)
    bh, bm, bl = parts(b)
    left = jnp.concatenate([ah, ah, am, am, ah, al], axis=dims[0][0]).astype(jnp.bfloat16)
    right = jnp.concatenate([bh, bm, bh, bm, bl, bh], axis=dims[1][0]).astype(jnp.bfloat16)
    return lax.dot_general(left, right, (dims, ((), ())), preferred_element_type=jnp.float32)

def factor_block(mat, tick):
    row_id = lax.broadcasted_iota(jnp.int32, (SUB, BLOCK), 0)
    lane_id = lax.broadcasted_iota(jnp.int32, (SUB, BLOCK), 1)
    steps = BLOCK // SUB
    d = mat
    uppers, invs = [], []
    g = None
    for s in range(steps):
        base = s * SUB
        rows = d[:SUB, :]
        eye = jnp.where(lane_id == row_id + base, 1.0, 0.0).astype(jnp.float32)
        if g is None:
            grows = eye
        else:
            grows = g[:SUB, :] + eye
        r = [jnp.broadcast_to(rows[j:j+1, :], (SUB, BLOCK)) for j in range(SUB)]
        q = [jnp.broadcast_to(grows[j:j+1, :], (SUB, BLOCK)) for j in range(SUB)]
        S = {}
        for j in range(SUB):
            for k in range(j, SUB):
                S[j, k] = jnp.broadcast_to(r[j][:, base+k:base+k+1], (SUB, BLOCK))
        for j in range(SUB):
            inv = lax.rsqrt(S[j, j])
            c = [None] * SUB
            for k in range(j + 1, SUB):
                c[k] = S[j, k] * inv
            r[j] = r[j] * inv
            q[j] = q[j] * inv
            for i in range(j + 1, SUB):
                for k in range(i, SUB):
                    S[i, k] = S[i, k] - c[i] * c[k]
                r[i] = r[i] - c[i] * r[j]
                q[i] = q[i] - c[i] * q[j]
        u = r[0]
        v = q[0]
        for j in range(1, SUB):
            u = jnp.where(row_id == j, r[j], u)
            v = jnp.where(row_id == j, q[j], v)
        u = jnp.where(lane_id >= row_id + base, u, 0.0)
        uppers.append(u)
        invs.append(v)
        tick()
        if s + 1 < steps:
            both = jnp.concatenate([u, v], axis=1)
            upd = mm6(u, both, ((0,), (0,)))
            d = d[SUB:, :] - upd[base+SUB:, :BLOCK]
            g = -upd[base+SUB:, BLOCK:] if g is None else g[SUB:, :] - upd[base+SUB:, BLOCK:]
    return jnp.concatenate(uppers, 0), jnp.concatenate(invs, 0)


def factor_kernel(rows_n, cols_n, a_ref, pb_ref, l_ref, inv_ref, pr_ref, pc_ref, w, y,
                  own, d_send, d_recv, x_send, x_recv, s_send, s_recv, c_send, c_recv, b_send, b_recv):
    n = w.shape[0]
    chips = rows_n // 2
    piece = n // rows_n
    tall = pb_ref.shape[0]
    block_rows = pr_ref.shape[0]
    ratio = pc_ref.shape[0] // block_rows
    r = lax.axis_index("row")
    c = lax.axis_index("col")
    z = r // 2
    k = lax.rem(r, 2)
    sibling = z * 2 + (1 - k)

    mine_a = pltpu.make_async_copy(a_ref, w.at[pl.ds(pl.multiple_of(r * piece, piece), piece)], own.at[0])
    mine_b = pltpu.make_async_copy(pb_ref, pr_ref.at[pl.ds(pl.multiple_of(c * tall, tall), tall)], own.at[1])
    mine_a.start()
    mine_b.start()
    barrier = pltpu.get_barrier_semaphore()
    for step in range(1, rows_n):
        pl.semaphore_signal(barrier, inc=1, device_id=(lax.rem(r + step, rows_n), c), device_id_type=MESH)
    for step in range(1, cols_n):
        pl.semaphore_signal(barrier, inc=1, device_id=(r, lax.rem(c + step, cols_n)), device_id_type=MESH)
    mine_a.wait()
    mine_b.wait()
    pl.semaphore_wait(barrier, rows_n + cols_n - 2)

    messages = []
    for p in range(chips):
        lo = p * 2 * piece // BLOCK * BLOCK
        if p == 0:
            messages.append((0, 0, BLOCK))
            lo = BLOCK
        if lo < n:
            messages.append((p, lo, n))

    def diag_copy(m, row, to_row, send, recv):
        p, lo, hi = messages[m]
        part = w.at[pl.ds(pl.multiple_of(row * piece, piece), piece), lo:hi]
        return pltpu.make_async_remote_copy(src_ref=part, dst_ref=part, send_sem=send, recv_sem=recv,
                                            device_id=(to_row, c), device_id_type=MESH)

    def along(m, step):
        to = lax.rem(z + step, chips) * 2 + k
        return diag_copy(m, r, to, d_send.at[m, step - 1], d_recv.at[m])

    def across(m):
        return diag_copy(m, messages[m][0] * 2 + k, sibling, x_send.at[m], x_recv.at[m])

    for m in range(len(messages)):
        @pl.when(z == messages[m][0])
        def _():
            for step in range(1, chips):
                along(m, step).start()

    passed = set()

    def pass_across(m):
        if m in passed:
            return
        passed.add(m)

        @pl.when(z != messages[m][0])
        def _():
            diag_copy(m, messages[m][0] * 2 + k, sibling, d_send.at[m, 0], d_recv.at[m]).wait_recv()
        across(m).start()

    def have(m):
        pass_across(m)
        part = diag_copy(m, messages[m][0] * 2 + (1 - k), sibling, x_send.at[m], x_recv.at[m])
        part.wait_recv()

    def in_row(step):
        part = pr_ref.at[pl.ds(pl.multiple_of(c * tall, tall), tall)]
        return pltpu.make_async_remote_copy(
            src_ref=part, dst_ref=part, send_sem=s_send.at[step - 1], recv_sem=s_recv.at[step - 1],
            device_id=(r, lax.rem(c - step + cols_n, cols_n)), device_id_type=MESH)

    def in_row_wait(step):
        part = pr_ref.at[pl.ds(pl.multiple_of(lax.rem(c + step, cols_n) * tall, tall), tall)]
        pltpu.make_async_remote_copy(
            src_ref=part, dst_ref=part, send_sem=s_send.at[step - 1], recv_sem=s_recv.at[step - 1],
            device_id=(r, lax.rem(c + step, cols_n)), device_id_type=MESH).wait_recv()

    home = c * ratio // 2

    def piece_at(j, core):
        first = lax.rem(c + j, cols_n) * tall
        base = core * block_rows if ratio == 2 else 0
        return pl.multiple_of(base + first, tall)

    def line_copy(j, to, send, recv, core):
        part = pc_ref.at[pl.ds(piece_at(j, core), tall)]
        return pltpu.make_async_remote_copy(src_ref=part, dst_ref=part, send_sem=send, recv_sem=recv,
                                            device_id=(to, c), device_id_type=MESH)

    def down(j):
        return line_copy(j, r + 2, c_send.at[j], c_recv.at[j], k)

    def swap(j, core):
        return line_copy(j, sibling, b_send.at[j], b_recv.at[j], core)

    holds = (z >= home) if ratio == 2 else (z >= home) & (lax.rem(c, 2) == k)
    takes = (z >= home) if ratio == 2 else (z >= home) & (lax.rem(c, 2) != k)

    def line_step(j, hop):
        @pl.when((z - home == hop) & holds)
        def _():
            if hop == 0:
                first = pl.multiple_of(lax.rem(c + j, cols_n) * tall, tall)
                pc_ref[pl.ds(piece_at(j, k), tall), :] = pr_ref[pl.ds(first, tall), :]
            else:
                down(j).wait_recv()
            @pl.when(z < chips - 1)
            def _():
                down(j).start()
            swap(j, k).start()

    ticks = n // SUB
    actions = {}
    span = cols_n + chips - 1
    for m in range(1, len(messages)):
        actions.setdefault(4 * m - 1, []).append(functools.partial(pass_across, m))
    for t in range(span):
        at = 2 + t * (ticks - 8) // (span - 1)
        if 0 < t < cols_n:
            actions.setdefault(at, []).append(functools.partial(in_row_wait, t))
        for j in range(cols_n):
            hop = t - j
            if 0 <= hop < chips:
                actions.setdefault(at, []).append(functools.partial(line_step, j, hop))
    count = [0]

    def tick():
        for action in actions.get(count[0], ()):
            action()
        count[0] += 1

    pass_across(0)
    for step in range(1, cols_n):
        in_row(step).start()
    y[...] = jnp.zeros_like(y)
    l_ref[...] = jnp.zeros_like(l_ref)
    have(0)
    waited = {0}
    for p in range(n // BLOCK):
        lo, hi = p * BLOCK, (p + 1) * BLOCK
        for m in range(len(messages)):
            if m not in waited and messages[m][0] * 2 * piece < hi and (p or messages[m][1] == 0):
                have(m)
                waited.add(m)
        now = w[lo:hi, lo:] if p else w[lo:hi, lo:hi]
        if p:
            before = l_ref[lo:, :lo]
            now = now - mm6(l_ref[lo:hi, :lo], before, ((1,), (1,)))
        u, v = factor_block(now[:, :BLOCK], tick)
        l_ref[lo:hi, lo:hi] = u.T
        if p:
            left = mm6(l_ref[lo:hi, :lo], y[:lo, :lo], ((1,), (0,)))
            y[lo:hi, :lo] = -mm6(v, left, ((1,), (0,)))
        y[lo:hi, lo:hi] = v
        if hi < n:
            if p == 0:
                for m in range(len(messages)):
                    if m not in waited and messages[m][0] * 2 * piece < hi:
                        have(m)
                        waited.add(m)
                rest = w[lo:hi, hi:]
            else:
                rest = now[:, BLOCK:]
            l_ref[hi:, lo:hi] = mm6(v, rest, ((1,), (0,))).T
    inv_ref[...] = y[...]

    for m in range(len(messages)):
        @pl.when(z == messages[m][0])
        def _():
            for step in range(1, chips):
                along(m, step).wait_send()
        across(m).wait_send()
    for step in range(1, cols_n):
        in_row(step).wait_send()
    for j in range(cols_n):
        @pl.when(holds)
        def _():
            @pl.when(z < chips - 1)
            def _():
                down(j).wait_send()
            swap(j, k).wait_send()

        @pl.when(takes)
        def _():
            swap(j, 1 - k).wait_recv()


def split(x):
    high = x.astype(jnp.bfloat16)
    return high, (x - high.astype(jnp.float32)).astype(jnp.bfloat16)


def left_parts(x, axis):
    high, low = split(x)
    return jnp.concatenate([high, high, low], axis=axis)


def right_parts(x, axis):
    high, low = split(x)
    return jnp.concatenate([high, low, high], axis=axis)


def dot(a, b, dims):
    return lax.dot_general(a, b, (dims, ((), ())), preferred_element_type=jnp.float32)


ROWS = ((1,), (0,))
COLS = ((1,), (1,))


def update_kernel(wide, deep, l_ref, pr_ref, pc_ref, inv_ref, top_ref, rest_ref, tr_ref,
                  l_out, below_ref, top_out, rest_out, tr_out, xr, xc, iv, iv_top, sem):
    t = pl.program_id(0)
    r = lax.axis_index("row")
    c = lax.axis_index("col")
    n = inv_ref.shape[0]
    half = n // 2
    tall = below_ref.shape[0]

    @pl.when(t == 0)
    def _():
        pltpu.make_async_copy(l_ref, l_out, sem).start()
        inv = right_parts(inv_ref[...], 1)
        xr[...] = left_parts(dot(left_parts(pr_ref[...], 1), inv, COLS), 1)
        xc[...] = right_parts(dot(left_parts(pc_ref[...], 1), inv, COLS), 1)
        own = pr_ref[pl.ds(pl.multiple_of(c * tall, tall), tall), :]
        below_ref[...] = dot(left_parts(own, 1), inv, COLS)
        iv[...] = left_parts(inv_ref[half:, :], 1)
        iv_top[...] = left_parts(inv_ref[:half, :half], 1)

    @pl.when(t < wide)
    def _():
        top = top_ref[...]
        upper = dot(iv_top[...], right_parts(top[:half], 0), ROWS)
        lower = dot(iv[...], right_parts(top, 0), ROWS)
        top_out[:half, :] = upper
        top_out[half:, :] = lower
        solved = right_parts(jnp.concatenate([upper, lower], 0), 0)
        rest_out[...] = rest_ref[...] - dot(xr[...], solved, ROWS)

    @pl.when(t >= wide)
    def _():
        height, width = tr_ref.shape
        at = pl.ds(pl.multiple_of((t - wide) * width, width), width)
        product = dot(xr[...], xc[at, :], COLS)
        row = r * height + lax.broadcasted_iota(jnp.int32, (height, width), 0)
        col = (c * deep + (t - wide)) * width + lax.broadcasted_iota(jnp.int32, (height, width), 1)
        tr_out[...] = jnp.where(col <= row, tr_ref[...] - product, tr_ref[...])

    @pl.when(t == wide + deep - 1)
    def _():
        pltpu.make_async_copy(l_ref, l_out, sem).wait()


def tile_of(size):
    for width in (512, 384, 256, 128):
        if size % width == 0:
            return width
    return size


def shards(rows_n, cols_n, panel_diag, panel_below, trailing, recon_top, recon_rest):
    n = panel_diag.shape[1]
    height, across = trailing.shape
    slopes = recon_top.shape[1]
    f32 = jnp.float32
    whole = pl.BlockSpec(memory_space=pltpu.VMEM)
    chips = rows_n // 2
    dma = pltpu.SemaphoreType.DMA
    diag_factor, inverse, row_panel, col_panel = pl.pallas_call(
        functools.partial(factor_kernel, rows_n, cols_n),
        out_shape=[jax.ShapeDtypeStruct((n, n), f32), jax.ShapeDtypeStruct((n, n), f32),
                   jax.ShapeDtypeStruct((height, n), f32), jax.ShapeDtypeStruct((across, n), f32)],
        in_specs=[pl.BlockSpec(memory_space=pl.ANY)] * 2,
        out_specs=[whole] * 4,
        scratch_shapes=[pltpu.VMEM((n, n), f32), pltpu.VMEM((n, n), f32),
                        dma((2,)), dma((chips + 1, chips - 1)), dma((chips + 1,)), dma((chips + 1,)), dma((chips + 1,)),
                        dma((cols_n - 1,)), dma((cols_n - 1,)), dma((cols_n,)), dma((cols_n,)),
                        dma((cols_n,)), dma((cols_n,))],
        compiler_params=pltpu.CompilerParams(collective_id=0, has_side_effects=True, vmem_limit_bytes=58 * 2**20),
        name="factor",
    )(panel_diag, panel_below)

    tile, strip = tile_of(slopes), tile_of(across)
    wide, deep = slopes // tile, across // strip
    bf16 = jnp.bfloat16
    recon_at = lambda t: (0, jnp.minimum(t, wide - 1))
    trail_at = lambda t: (0, jnp.maximum(t - wide, 0))
    diag_out, below, top_solved, rest_new, trailing_new = pl.pallas_call(
        functools.partial(update_kernel, wide, deep),
        grid=(wide + deep,),
        out_shape=[jax.ShapeDtypeStruct((n, n), f32), jax.ShapeDtypeStruct(panel_below.shape, f32),
                   jax.ShapeDtypeStruct(recon_top.shape, f32),
                   jax.ShapeDtypeStruct(recon_rest.shape, f32), jax.ShapeDtypeStruct(trailing.shape, f32)],
        in_specs=[whole, whole, whole, whole, pl.BlockSpec((n, tile), recon_at),
                  pl.BlockSpec((height, tile), recon_at), pl.BlockSpec((height, strip), trail_at)],
        out_specs=[pl.BlockSpec(memory_space=pl.ANY), whole, pl.BlockSpec((n, tile), recon_at),
                   pl.BlockSpec((height, tile), recon_at), pl.BlockSpec((height, strip), trail_at)],
        scratch_shapes=[pltpu.VMEM((height, 3 * n), bf16), pltpu.VMEM((across, 3 * n), bf16),
                        pltpu.VMEM((n - n // 2, 3 * n), bf16), pltpu.VMEM((n // 2, 3 * (n // 2)), bf16), dma],
        compiler_params=pltpu.CompilerParams(vmem_limit_bytes=57 * 2**20),
        name="update",
    )(diag_factor, row_panel, col_panel, inverse, recon_top, recon_rest, trailing)
    return (diag_out, below, trailing_new, top_solved, rest_new)


def solution(mesh):
    rows_n, cols_n = mesh.shape["row"], mesh.shape["col"]
    placed = (
        P("row", None),
        P(("row", "col"), None),
        P("row", "col"),
        P(None, "col"),
        P("row", "col"),
    )
    return jax.shard_map(
        functools.partial(shards, rows_n, cols_n),
        mesh=mesh,
        in_specs=placed,
        out_specs=(P(), P(("row", "col"), None), P("row", "col"), P(None, "col"), P("row", "col")),
        check_vma=False,
    )
```

```python
import functools

import jax
import jax.numpy as jnp
from jax import lax
from jax.experimental import pallas as pl
from jax.experimental.pallas import tpu as pltpu
from jax.sharding import PartitionSpec as P

HI = lax.Precision.HIGHEST
MESH = pl.DeviceIdType.MESH
BLOCK = 128
SUB = 8
CUTS = 2


def rounded(x):
    return x.astype(jnp.bfloat16).astype(jnp.float32)

def mm6(a, b, dims):
    def parts(x):
        high = rounded(x)
        mid = rounded(x - high)
        return high, mid, (x - high) - mid
    ah, am, al = parts(a)
    bh, bm, bl = parts(b)
    left = jnp.concatenate([ah, ah, am, am, ah, al], axis=dims[0][0]).astype(jnp.bfloat16)
    right = jnp.concatenate([bh, bm, bh, bm, bl, bh], axis=dims[1][0]).astype(jnp.bfloat16)
    return lax.dot_general(left, right, (dims, ((), ())), preferred_element_type=jnp.float32)

def factor_block(mat, tick):
    row_id = lax.broadcasted_iota(jnp.int32, (SUB, BLOCK), 0)
    lane_id = lax.broadcasted_iota(jnp.int32, (SUB, BLOCK), 1)
    steps = BLOCK // SUB
    d = mat
    uppers, invs = [], []
    g = None
    for s in range(steps):
        base = s * SUB
        rows = d[:SUB, :]
        eye = jnp.where(lane_id == row_id + base, 1.0, 0.0).astype(jnp.float32)
        if g is None:
            grows = eye
        else:
            grows = g[:SUB, :] + eye
        r = [jnp.broadcast_to(rows[j:j+1, :], (SUB, BLOCK)) for j in range(SUB)]
        q = [jnp.broadcast_to(grows[j:j+1, :], (SUB, BLOCK)) for j in range(SUB)]
        S = {}
        for j in range(SUB):
            for k in range(j, SUB):
                S[j, k] = jnp.broadcast_to(r[j][:, base+k:base+k+1], (SUB, BLOCK))
        for j in range(SUB):
            inv = lax.rsqrt(S[j, j])
            c = [None] * SUB
            for k in range(j + 1, SUB):
                c[k] = S[j, k] * inv
            r[j] = r[j] * inv
            q[j] = q[j] * inv
            for i in range(j + 1, SUB):
                for k in range(i, SUB):
                    S[i, k] = S[i, k] - c[i] * c[k]
                r[i] = r[i] - c[i] * r[j]
                q[i] = q[i] - c[i] * q[j]
        u = r[0]
        v = q[0]
        for j in range(1, SUB):
            u = jnp.where(row_id == j, r[j], u)
            v = jnp.where(row_id == j, q[j], v)
        u = jnp.where(lane_id >= row_id + base, u, 0.0)
        uppers.append(u)
        invs.append(v)
        tick()
        if s + 1 < steps:
            both = jnp.concatenate([u, v], axis=1)
            upd = mm6(u, both, ((0,), (0,)))
            d = d[SUB:, :] - upd[base+SUB:, :BLOCK]
            g = -upd[base+SUB:, BLOCK:] if g is None else g[SUB:, :] - upd[base+SUB:, BLOCK:]
    return jnp.concatenate(uppers, 0), jnp.concatenate(invs, 0)


def factor_kernel(rows_n, cols_n, a_ref, pb_ref, l_ref, inv_ref, pr_ref, pc_ref, w, y,
                  own, d_send, d_recv, x_send, x_recv, s_send, s_recv, c_send, c_recv, b_send, b_recv):
    n = w.shape[0]
    chips = rows_n // 2
    piece = n // rows_n
    tall = pb_ref.shape[0]
    short = tall // CUTS
    block_rows = pr_ref.shape[0]
    ratio = pc_ref.shape[0] // block_rows
    r = lax.axis_index("row")
    c = lax.axis_index("col")
    z = r // 2
    k = lax.rem(r, 2)
    sibling = z * 2 + (1 - k)

    mine_a = pltpu.make_async_copy(a_ref, w.at[pl.ds(pl.multiple_of(r * piece, piece), piece)], own.at[0])
    mine_b = pltpu.make_async_copy(pb_ref, pr_ref.at[pl.ds(pl.multiple_of(c * tall, tall), tall)], own.at[1])
    mine_a.start()
    mine_b.start()
    barrier = pltpu.get_barrier_semaphore()
    for step in range(1, rows_n):
        pl.semaphore_signal(barrier, inc=1, device_id=(lax.rem(r + step, rows_n), c), device_id_type=MESH)
    for step in range(1, cols_n):
        pl.semaphore_signal(barrier, inc=1, device_id=(r, lax.rem(c + step, cols_n)), device_id_type=MESH)
    mine_a.wait()
    mine_b.wait()
    pl.semaphore_wait(barrier, rows_n + cols_n - 2)

    messages = []
    for p in range(chips):
        lo = p * 2 * piece // BLOCK * BLOCK
        if p == 0:
            messages.append((0, 0, BLOCK))
            lo = BLOCK
        if lo < n:
            messages.append((p, lo, n))

    def diag_copy(m, row, to_row, send, recv):
        p, lo, hi = messages[m]
        part = w.at[pl.ds(pl.multiple_of(row * piece, piece), piece), lo:hi]
        return pltpu.make_async_remote_copy(src_ref=part, dst_ref=part, send_sem=send, recv_sem=recv,
                                            device_id=(to_row, c), device_id_type=MESH)

    def across(m):
        return diag_copy(m, messages[m][0] * 2 + k, sibling, x_send.at[m], x_recv.at[m])

    def direct(step):
        to = lax.rem(z + step, chips) * 2 + k
        return diag_copy(0, r, to, d_send.at[0, step - 1], d_recv.at[0])

    def onward(m, way):
        row = messages[m][0] * 2 + k
        return diag_copy(m, row, r + 2 - 4 * way, d_send.at[m, way], d_recv.at[m])

    def goes(m, way):
        p = messages[m][0]
        return (z >= p) & (z < chips - 1) if way == 0 else (z <= p) & (z > 0)

    def pass_on(m):
        for way in range(2):
            @pl.when(goes(m, way))
            def _():
                onward(m, way).start()
        across(m).start()

    @pl.when(z == 0)
    def _():
        for step in range(1, chips):
            direct(step).start()
        across(0).start()
    for m in range(1, len(messages)):
        @pl.when(z == messages[m][0])
        def _():
            pass_on(m)

    passed = set()

    def forward(m, hop):
        if (m, hop) in passed:
            return
        passed.add((m, hop))
        p = messages[m][0]

        @pl.when((z == p + hop) | (z == p - hop))
        def _():
            onward(m, 0).wait_recv()
            if m == 0:
                across(0).start()
            else:
                pass_on(m)

    def have(m):
        for hop in range(1, chips):
            forward(m, hop)
        part = diag_copy(m, messages[m][0] * 2 + (1 - k), sibling, x_send.at[m], x_recv.at[m])
        part.wait_recv()

    def in_row(step):
        part = pr_ref.at[pl.ds(pl.multiple_of(c * tall, tall), tall)]
        return pltpu.make_async_remote_copy(
            src_ref=part, dst_ref=part, send_sem=s_send.at[step - 1], recv_sem=s_recv.at[step - 1],
            device_id=(r, lax.rem(c - step + cols_n, cols_n)), device_id_type=MESH)

    def in_row_wait(step):
        part = pr_ref.at[pl.ds(pl.multiple_of(lax.rem(c + step, cols_n) * tall, tall), tall)]
        pltpu.make_async_remote_copy(
            src_ref=part, dst_ref=part, send_sem=s_send.at[step - 1], recv_sem=s_recv.at[step - 1],
            device_id=(r, lax.rem(c + step, cols_n)), device_id_type=MESH).wait_recv()

    home = c * ratio // 2

    def piece_at(j, core):
        first = lax.rem(c + j // CUTS, cols_n) * tall + j % CUTS * short
        base = core * block_rows if ratio == 2 else 0
        return pl.multiple_of(base + first, short)

    def line_copy(j, to, send, recv, core):
        part = pc_ref.at[pl.ds(piece_at(j, core), short)]
        return pltpu.make_async_remote_copy(src_ref=part, dst_ref=part, send_sem=send, recv_sem=recv,
                                            device_id=(to, c), device_id_type=MESH)

    def down(j):
        return line_copy(j, r + 2, c_send.at[j], c_recv.at[j], k)

    def swap(j, core):
        return line_copy(j, sibling, b_send.at[j], b_recv.at[j], core)

    holds = (z >= home) if ratio == 2 else (z >= home) & (lax.rem(c, 2) == k)
    takes = (z >= home) if ratio == 2 else (z >= home) & (lax.rem(c, 2) != k)

    def line_step(j, hop):
        @pl.when((z - home == hop) & holds)
        def _():
            if hop == 0:
                first = pl.multiple_of(lax.rem(c + j // CUTS, cols_n) * tall + j % CUTS * short, short)
                pc_ref[pl.ds(piece_at(j, k), short), :] = pr_ref[pl.ds(first, short), :]
            else:
                down(j).wait_recv()
            @pl.when(z < chips - 1)
            def _():
                down(j).start()
            swap(j, k).start()

    ticks = n // SUB
    actions = {}
    span = CUTS * cols_n + chips - 1
    for m in range(1, len(messages)):
        for hop in range(1, chips):
            actions.setdefault(3 * m + 3 * hop - 3, []).append(functools.partial(forward, m, hop))
    for t in range(span):
        at = 2 + t * (ticks - 4) // (span - 1)
        if t % CUTS == 0 and 0 < t // CUTS < cols_n:
            actions.setdefault(at, []).append(functools.partial(in_row_wait, t // CUTS))
        for j in range(CUTS * cols_n):
            hop = t - j
            if 0 <= hop < chips:
                actions.setdefault(at, []).append(functools.partial(line_step, j, hop))
    count = [0]

    def tick():
        for action in actions.get(count[0], ()):
            action()
        count[0] += 1

    for hop in range(1, chips):
        forward(0, hop)
    for step in range(1, cols_n):
        in_row(step).start()
    y[...] = jnp.zeros_like(y)
    l_ref[...] = jnp.zeros_like(l_ref)
    have(0)
    waited = {0}
    for p in range(n // BLOCK):
        lo, hi = p * BLOCK, (p + 1) * BLOCK
        for m in range(len(messages)):
            if m not in waited and messages[m][0] * 2 * piece < hi and (p or messages[m][1] == 0):
                have(m)
                waited.add(m)
        now = w[lo:hi, lo:] if p else w[lo:hi, lo:hi]
        if p:
            before = l_ref[lo:, :lo]
            now = now - mm6(l_ref[lo:hi, :lo], before, ((1,), (1,)))
        u, v = factor_block(now[:, :BLOCK], tick)
        l_ref[lo:hi, lo:hi] = u.T
        if p:
            left = mm6(l_ref[lo:hi, :lo], y[:lo, :lo], ((1,), (0,)))
            y[lo:hi, :lo] = -mm6(v, left, ((1,), (0,)))
        y[lo:hi, lo:hi] = v
        if hi < n:
            if p == 0:
                for m in range(len(messages)):
                    if m not in waited and messages[m][0] * 2 * piece < hi:
                        have(m)
                        waited.add(m)
                rest = w[lo:hi, hi:]
            else:
                rest = now[:, BLOCK:]
            l_ref[hi:, lo:hi] = mm6(v, rest, ((1,), (0,))).T
    inv_ref[...] = y[...]

    @pl.when(z == 0)
    def _():
        for step in range(1, chips):
            direct(step).wait_send()
    for m in range(len(messages)):
        if m:
            for way in range(2):
                @pl.when(goes(m, way))
                def _():
                    onward(m, way).wait_send()
        across(m).wait_send()
    for step in range(1, cols_n):
        in_row(step).wait_send()
    for j in range(CUTS * cols_n):
        @pl.when(holds)
        def _():
            @pl.when(z < chips - 1)
            def _():
                down(j).wait_send()
            swap(j, k).wait_send()

        @pl.when(takes)
        def _():
            swap(j, 1 - k).wait_recv()


def split(x):
    high = x.astype(jnp.bfloat16)
    return high, (x - high.astype(jnp.float32)).astype(jnp.bfloat16)


def left_parts(x, axis):
    high, low = split(x)
    return jnp.concatenate([high, high, low], axis=axis)


def right_parts(x, axis):
    high, low = split(x)
    return jnp.concatenate([high, low, high], axis=axis)


def dot(a, b, dims):
    return lax.dot_general(a, b, (dims, ((), ())), preferred_element_type=jnp.float32)


ROWS = ((1,), (0,))
COLS = ((1,), (1,))


def update_kernel(wide, deep, l_ref, pr_ref, pc_ref, inv_ref, top_ref, rest_ref, tr_ref,
                  l_out, below_ref, top_out, rest_out, tr_out, weights, iv_top, solved, sem):
    t = pl.program_id(0)
    r = lax.axis_index("row")
    c = lax.axis_index("col")
    n = inv_ref.shape[0]
    half = n // 2
    tall = below_ref.shape[0]

    @pl.when(t == 0)
    def _():
        pltpu.make_async_copy(l_ref, l_out, sem).start()
        inv = inv_ref[...]
        iv_top[...] = left_parts(inv[:half, :half], 1)
        weights[:half, :] = left_parts(inv[half:, :], 1)
        solved[...] = dot(left_parts(pr_ref[...], 1), right_parts(inv, 1), COLS)
        below_ref[...] = solved[pl.ds(pl.multiple_of(c * tall, tall), tall), :]
        weights[half:, :] = left_parts(dot(left_parts(solved[...], 1), right_parts(inv, 0), ROWS), 1)

    @pl.when(t < wide)
    def _():
        parts = right_parts(top_ref[:half, :], 0)
        top_out[:half, :] = dot(iv_top[...], parts, ROWS)
        parts = right_parts(top_ref[...], 0)
        top_out[half:, :] = dot(weights[:half, :], parts, ROWS)
        rest_out[...] = rest_ref[...] - dot(weights[half:, :], parts, ROWS)

    @pl.when(t >= wide)
    def _():
        height, width = tr_ref.shape
        at = pl.ds(pl.multiple_of((t - wide) * width, width), width)
        product = dot(weights[half:, :], right_parts(pc_ref[at, :], 1), COLS)
        row = r * height + lax.broadcasted_iota(jnp.int32, (height, width), 0)
        col = (c * deep + (t - wide)) * width + lax.broadcasted_iota(jnp.int32, (height, width), 1)
        tr_out[...] = jnp.where(col <= row, tr_ref[...] - product, tr_ref[...])

    @pl.when(t == wide + deep - 1)
    def _():
        pltpu.make_async_copy(l_ref, l_out, sem).wait()


def tile_of(size):
    for width in (512, 384, 256, 128):
        if size % width == 0:
            return width
    return size


def shards(rows_n, cols_n, panel_diag, panel_below, trailing, recon_top, recon_rest):
    n = panel_diag.shape[1]
    height, across = trailing.shape
    slopes = recon_top.shape[1]
    f32 = jnp.float32
    whole = pl.BlockSpec(memory_space=pltpu.VMEM)
    chips = rows_n // 2
    dma = pltpu.SemaphoreType.DMA
    diag_factor, inverse, row_panel, col_panel = pl.pallas_call(
        functools.partial(factor_kernel, rows_n, cols_n),
        out_shape=[jax.ShapeDtypeStruct((n, n), f32), jax.ShapeDtypeStruct((n, n), f32),
                   jax.ShapeDtypeStruct((height, n), f32), jax.ShapeDtypeStruct((across, n), f32)],
        in_specs=[pl.BlockSpec(memory_space=pl.ANY)] * 2,
        out_specs=[whole] * 4,
        scratch_shapes=[pltpu.VMEM((n, n), f32), pltpu.VMEM((n, n), f32),
                        dma((2,)), dma((chips + 1, chips - 1)), dma((chips + 1,)), dma((chips + 1,)), dma((chips + 1,)),
                        dma((cols_n - 1,)), dma((cols_n - 1,)), dma((CUTS * cols_n,)), dma((CUTS * cols_n,)),
                        dma((CUTS * cols_n,)), dma((CUTS * cols_n,))],
        compiler_params=pltpu.CompilerParams(collective_id=0, has_side_effects=True, vmem_limit_bytes=58 * 2**20),
        name="factor",
    )(panel_diag, panel_below)

    tile, strip = tile_of(slopes), tile_of(across)
    wide, deep = slopes // tile, across // strip
    bf16 = jnp.bfloat16
    recon_at = lambda t: (0, jnp.minimum(t, wide - 1))
    trail_at = lambda t: (0, jnp.maximum(t - wide, 0))
    diag_out, below, top_solved, rest_new, trailing_new = pl.pallas_call(
        functools.partial(update_kernel, wide, deep),
        grid=(wide + deep,),
        out_shape=[jax.ShapeDtypeStruct((n, n), f32), jax.ShapeDtypeStruct(panel_below.shape, f32),
                   jax.ShapeDtypeStruct(recon_top.shape, f32),
                   jax.ShapeDtypeStruct(recon_rest.shape, f32), jax.ShapeDtypeStruct(trailing.shape, f32)],
        in_specs=[whole, whole, whole, whole, pl.BlockSpec((n, tile), recon_at),
                  pl.BlockSpec((height, tile), recon_at), pl.BlockSpec((height, strip), trail_at)],
        out_specs=[pl.BlockSpec(memory_space=pl.ANY), whole, pl.BlockSpec((n, tile), recon_at),
                   pl.BlockSpec((height, tile), recon_at), pl.BlockSpec((height, strip), trail_at)],
        scratch_shapes=[pltpu.VMEM((n - n // 2 + height, 3 * n), bf16), pltpu.VMEM((n // 2, 3 * (n // 2)), bf16),
                        pltpu.VMEM((height, n), f32), dma],
        compiler_params=pltpu.CompilerParams(vmem_limit_bytes=57 * 2**20),
        name="update",
    )(diag_factor, row_panel, col_panel, inverse, recon_top, recon_rest, trailing)
    return (diag_out, below, trailing_new, top_solved, rest_new)


def solution(mesh):
    rows_n, cols_n = mesh.shape["row"], mesh.shape["col"]
    placed = (
        P("row", None),
        P(("row", "col"), None),
        P("row", "col"),
        P(None, "col"),
        P("row", "col"),
    )
    return jax.shard_map(
        functools.partial(shards, rows_n, cols_n),
        mesh=mesh,
        in_specs=placed,
        out_specs=(P(), P(("row", "col"), None), P("row", "col"), P(None, "col"), P("row", "col")),
        check_vma=False,
    )
```
